32 devices in a mesh: group: 2 (over y), ctx: 8 (over z, x), tp: 2 (over core).
Axes of the slice: x: 2, y: 2, z: 4, core: 2. Of those that a mesh axis runs over, the one named last changes fastest.
Arguments:
- hidden: bfloat16 [256, 16384], P(('group', 'ctx')), parts along dimension 0, may hold values from -6 to 6
- q_base: bfloat16 [256, 8192], P(('group', 'ctx'), 'tp'), parts along dimension 0, may hold values from -6 to 6
- adapter_down: bfloat16 [16, 16384, 64], P(('group', 'ctx')), parts along dimension 0, may hold values from -0.046875 to 0.046875
- adapter_up: bfloat16 [16, 64, 8192], P(('group', 'ctx'), None, 'tp'), parts along dimension 0, may hold values from -0.75 to 0.75
- adapter_owner: int32 [2], P('group'), parts along dimension 0, may hold values from 0 to 7
- turn_start: int32 [2], P('group'), parts along dimension 0, may hold values from 512 to 2047
- shard_lengths: int32 [16], P('group'), parts along dimension 0, may hold values from 1 to 64, 384 in all
- stored_keys: bfloat16 [1024, 512], P(('group', 'ctx'), 'tp'), parts along dimension 0, may hold values from -250 to 250
- stored_values: bfloat16 [1024, 512], P(('group', 'ctx'), 'tp'), parts along dimension 0, may hold values from -6 to 6
- unrotated_turn_keys: bfloat16 [256, 512], P(('group', 'ctx'), 'tp'), parts along dimension 0, may hold values from -15 to 15
- incoming_values: bfloat16 [256, 512], P(('group', 'ctx'), 'tp'), parts along dimension 0, may hold values from -6 to 6
Outputs:
- attended: bfloat16 [256, 8192], P(('group', 'ctx'), 'tp'), parts along dimension 0
The draws below stay inside these ranges and needn't reach their ends.
There are 2 independent parts, one for each index of `group`. The reference program is written for one: setup_inputs(seed, part) draws one part's arguments, and reference() takes and returns one part's arrays. A program takes and returns all parts, laid end to end along the dimension named above; each array names one. Nothing has to cross between parts.
Inputs may be any that keep to these rules, and one draw needn't show every extreme that they name: The used slots of shard s are its slots 0 .. shard_lengths[s] - 1; some shard uses all 64.
All inputs are finite; a program needn't handle non-finite values.
Results may differ from the reference program's by a relative error of at most 0.019.
The reference program's roundings to bfloat16 on the way count: a program that leaves them out, or rounds other values in their place, can miss the bound.
Values may be sent and summed in bfloat16 or wider, within the bound.
A program may use at most 64 MiB of HBM per device.

```python
import math
import jax
import jax.numpy as jnp
import numpy as np
from jax import lax

D = 16384
QUERY_HEAD_COUNT = 64
KEY_VALUE_HEADS = 4
HEAD_SIZE = 128
RANK = 64
QUERY_PER_SHARD = 16
CACHE_PER_SHARD = 64
TURN_TOKENS = 128
CACHE_SLOTS_ALL = 512
N_CTX = 8


def draw_stored_keys(key, part):
    leading_key = jax.random.fold_in(jax.random.fold_in(key, 71), 0)
    drawn = jnp.clip(jax.random.normal(leading_key, (CACHE_SLOTS_ALL, KEY_VALUE_HEADS * HEAD_SIZE), jnp.float32) * 2.5, -15.0, 15.0)
    return drawn.astype(jnp.bfloat16)


def level_of(own_key, shape, shards, least, top_value):
    level, own = 1.0, jax.random.fold_in(own_key, 6)
    for axis_at, shards_of in shards:
        heights = jnp.exp(jax.random.uniform(jax.random.fold_in(own, axis_at), (shards_of,), jnp.float32, least / len(shards), top_value / len(shards)))
        level = level * jnp.repeat(heights, shape[axis_at] // shards_of).reshape([-1 if axis == axis_at else 1 for axis in range(len(shape))])
    return level


def split_up(number_of, total, most, lean):
    loads = [(1 << 20) // math.isqrt(grade ** lean) + 1 for grade in range(2, number_of + 1)]
    surplus, holding = total - most - (number_of - 1), [1] * (number_of - 1)
    while surplus > 0:
        free = [i for i in range(number_of - 1) if holding[i] < most]
        mass, remaining = sum([loads[i] for i in free]), surplus
        for i in free:
            extra = min(most - holding[i], max(1, remaining * loads[i] // mass), surplus)
            holding[i] = holding[i] + extra
            surplus = surplus - extra
    return np.array([most] + holding)


def ragged_sizes(key, count, total, limit, skew):
    if count == 2:
        one = jax.random.randint(key, (), max(1, total - limit), min(limit, total - 1) + 1)
        return jnp.stack([one, total - one])
    sizes = jnp.asarray(split_up(count, total, limit, skew), jnp.int32)
    twos = (count - 1) // 2
    donor, taker = sizes[1:1 + 2 * twos:2], sizes[2:2 + 2 * twos:2]
    room = jnp.minimum(donor - 1, limit - taker)
    moved = jax.random.randint(jax.random.fold_in(key, 1), (twos,), 0, 1 << 20) % (room + 1)
    sizes = sizes.at[1:1 + 2 * twos:2].set(donor - moved).at[2:2 + 2 * twos:2].set(taker + moved)
    return sizes[jax.random.permutation(jax.random.fold_in(key, 2), count)]


def gaussian(key, extent, width, most, cuts=(), kind=jnp.bfloat16):
    values = jax.random.normal(key, extent, jnp.float32) * width
    if len(cuts) > 0:
        values = level_of(key, extent, cuts, -0.22, 0.18) * values
    return jnp.clip(values, min=-most, max=most).astype(kind)


def setup_inputs(seed: int = 0, part: int = 0) -> dict:
    streams_of = jax.random.split(jax.random.key(seed), 12)
    part_keys = jax.random.split(jax.random.fold_in(streams_of[11], part), 12)
    return {
        "hidden": gaussian(part_keys[0], (TURN_TOKENS, D), 1.0, 6.0, ((0, 8),)),
        "q_base": gaussian(part_keys[1], (TURN_TOKENS, QUERY_HEAD_COUNT * HEAD_SIZE), 1.0, 6.0, ((0, 8), (1, 2))),
        "adapter_down": gaussian(part_keys[2], (N_CTX, D, RANK), D ** -0.5, 0.046875, ((0, 8),)),
        "adapter_up": gaussian(part_keys[3], (N_CTX, RANK, QUERY_HEAD_COUNT * HEAD_SIZE), RANK ** -0.5, 0.75, ((0, 8), (2, 2))),
        "adapter_owner": jax.random.randint(part_keys[4], (1,), 0, N_CTX).astype(jnp.int32),
        "turn_start": jax.random.randint(part_keys[5], (1,), CACHE_SLOTS_ALL, 4 * CACHE_SLOTS_ALL).astype(jnp.int32),
        "shard_lengths": ragged_sizes(part_keys[6], N_CTX, N_CTX * CACHE_PER_SHARD * 3 // 4, CACHE_PER_SHARD, 1).astype(jnp.int32),
        "stored_keys": draw_stored_keys(jax.random.fold_in(jax.random.fold_in(streams_of[11], part), 71), part),
        "stored_values": gaussian(part_keys[8], (CACHE_SLOTS_ALL, KEY_VALUE_HEADS * HEAD_SIZE), 1.0, 6.0, ((0, 8), (1, 2))),
        "unrotated_turn_keys": gaussian(part_keys[9], (TURN_TOKENS, KEY_VALUE_HEADS * HEAD_SIZE), 2.5, 15.0, ((0, 8), (1, 2))),
        "incoming_values": gaussian(part_keys[10], (TURN_TOKENS, KEY_VALUE_HEADS * HEAD_SIZE), 1.0, 6.0, ((0, 8), (1, 2))),
    }


def apply_rotary(values, token_positions, heads):
    half_dim = HEAD_SIZE // 2
    inverse = jnp.exp(jnp.arange(half_dim, dtype=jnp.float32) * (-2.0 * math.log(500000.0) / HEAD_SIZE))
    angles = token_positions.astype(jnp.float32)[:, None] * inverse[None, :]
    cosine = jnp.cos(angles)[:, None, :]
    sine = jnp.sin(angles)[:, None, :]
    shaped = values.reshape(values.shape[0], heads, HEAD_SIZE)
    first = shaped[..., :half_dim]
    second = shaped[..., half_dim:]
    turned = jnp.concatenate([first * cosine - second * sine, second * cosine + first * sine], axis=-1)
    return turned.reshape(values.shape[0], heads * HEAD_SIZE)

def reference(hidden, q_base, adapter_down, adapter_up, adapter_owner, turn_start, shard_lengths, stored_keys, stored_values, unrotated_turn_keys, incoming_values):
    adapter_a = adapter_down[adapter_owner[0]]
    adapter_b = adapter_up[adapter_owner[0]]
    lowrank = jnp.dot(hidden, adapter_a, preferred_element_type=jnp.float32).astype(jnp.bfloat16)
    adapter_delta = jnp.dot(lowrank, adapter_b, preferred_element_type=jnp.float32)
    token_positions = turn_start[0] + jnp.arange(TURN_TOKENS, dtype=jnp.int32)
    query_rows = apply_rotary(q_base.astype(jnp.float32) + 0.5 * adapter_delta, token_positions, QUERY_HEAD_COUNT).astype(jnp.bfloat16)
    rotated_turn_keys = apply_rotary(unrotated_turn_keys.astype(jnp.float32), token_positions, KEY_VALUE_HEADS).astype(jnp.bfloat16)
    key_head_rows = jnp.concatenate([stored_keys, rotated_turn_keys], axis=0).astype(jnp.float32).reshape(-1, KEY_VALUE_HEADS, HEAD_SIZE)
    value_head_rows = jnp.concatenate([stored_values, incoming_values], axis=0).astype(jnp.float32).reshape(-1, KEY_VALUE_HEADS, HEAD_SIZE)
    slot_index = jnp.arange(CACHE_SLOTS_ALL, dtype=jnp.int32)
    cache_used = slot_index % CACHE_PER_SHARD < shard_lengths[slot_index // CACHE_PER_SHARD]
    turn_index = jnp.arange(TURN_TOKENS, dtype=jnp.int32)
    score_scale = 1.0 / math.sqrt(HEAD_SIZE)
    block_list = query_rows.astype(jnp.float32).reshape(TURN_TOKENS // QUERY_PER_SHARD, QUERY_PER_SHARD, KEY_VALUE_HEADS, QUERY_HEAD_COUNT // KEY_VALUE_HEADS, HEAD_SIZE)
    firsts = jnp.arange(TURN_TOKENS // QUERY_PER_SHARD, dtype=jnp.int32) * QUERY_PER_SHARD

    def one_block(inputs):
        block, first = inputs
        scores = jnp.einsum('rhgd,khd->rhgk', block, key_head_rows) * score_scale
        mine = first + jnp.arange(QUERY_PER_SHARD, dtype=jnp.int32)
        turn_used = turn_index[None, :] <= mine[:, None]
        allowed = jnp.concatenate([jnp.broadcast_to(cache_used[None, :], (QUERY_PER_SHARD, CACHE_SLOTS_ALL)), turn_used], axis=1)
        allowed = allowed[:, None, None, :]
        highest = lax.optimization_barrier(jnp.max(jnp.where(allowed, scores, -1e+30), axis=-1))
        weights = jnp.where(allowed, jnp.exp(scores - highest[..., None]), 0.0)
        denominator = lax.optimization_barrier(jnp.sum(weights, axis=-1))
        rounded = lax.optimization_barrier(weights.astype(jnp.bfloat16)).astype(jnp.float32)
        numerator = jnp.einsum('rhgk,khd->rhgd', rounded, value_head_rows)
        return numerator / denominator[..., None]
    result = lax.map(one_block, (block_list, firsts))
    return result.reshape(TURN_TOKENS, QUERY_HEAD_COUNT * HEAD_SIZE).astype(jnp.bfloat16)
```

```python
import functools
import math

import jax
import jax.numpy as jnp
from jax import lax
from jax.experimental import pallas as pl
from jax.experimental.pallas import tpu as pltpu
from jax.sharding import PartitionSpec as P

HEAD_SIZE = 128


def spread(shard, axis, root):
    mine = lax.axis_index(axis) == root
    return lax.psum(jnp.where(mine, shard, jnp.zeros_like(shard)), axis)


def apply_rotary(values, token_positions, heads):
    half_dim = HEAD_SIZE // 2
    inverse = jnp.exp(
        jnp.arange(half_dim, dtype=jnp.float32) * (-2.0 * math.log(500000.0) / HEAD_SIZE)
    )
    angles = token_positions.astype(jnp.float32)[:, None] * inverse[None, :]
    cosine = jnp.cos(angles)[:, None, :]
    sine = jnp.sin(angles)[:, None, :]
    shaped = values.reshape(values.shape[0], heads, HEAD_SIZE)
    first = shaped[..., :half_dim]
    second = shaped[..., half_dim:]
    turned = jnp.concatenate(
        [first * cosine - second * sine, second * cosine + first * sine], axis=-1
    )
    return turned.reshape(values.shape[0], heads * HEAD_SIZE)


def shards(
    hidden,
    q_base,
    adapter_down,
    adapter_up,
    adapter_owner,
    turn_start,
    shard_lengths,
    stored_keys,
    stored_values,
    unrotated_turn_keys,
    incoming_values,
):
    holder = adapter_owner[0]
    slot_down = adapter_down[0]
    slot_up = adapter_up[0]
    got_down, got_up = (spread(slot_down, "ctx", holder), spread(slot_up, "ctx", holder))
    lowrank = jnp.dot(hidden, got_down, preferred_element_type=jnp.float32).astype(jnp.bfloat16)
    adapter_delta = jnp.dot(lowrank, got_up, preferred_element_type=jnp.float32)
    token_count = q_base.shape[0]
    slot_count = stored_keys.shape[0]
    shard_rows = token_count + slot_count
    ctx_size = lax.axis_size("ctx")
    myself = lax.axis_index("ctx")
    query_heads = q_base.shape[1] // HEAD_SIZE
    kv_heads = unrotated_turn_keys.shape[1] // HEAD_SIZE
    groups = query_heads // kv_heads
    local_tokens = jnp.arange(token_count, dtype=jnp.int32)
    token_positions = turn_start[0] + myself * token_count + local_tokens
    query_rows = apply_rotary(
        q_base.astype(jnp.float32) + 0.5 * adapter_delta, token_positions, query_heads
    ).astype(jnp.bfloat16)
    rotated_turn_keys = apply_rotary(
        unrotated_turn_keys.astype(jnp.float32), token_positions, kv_heads
    ).astype(jnp.bfloat16)
    grouped = query_rows.reshape(token_count, kv_heads, groups, HEAD_SIZE)
    key_here = jnp.concatenate([stored_keys, rotated_turn_keys], axis=0)
    value_here = jnp.concatenate([stored_values, incoming_values], axis=0)
    mine = myself * token_count + local_tokens
    score_scale = 1.0 / math.sqrt(HEAD_SIZE)
    shard_ids = jnp.arange(ctx_size, dtype=jnp.int32)

    def absorb(state, key_block, value_block, start):
        highest, denominator, accum = state
        row_count = key_block.shape[0]
        global_rows = start + jnp.arange(row_count, dtype=jnp.int32)
        owner_shard = global_rows // shard_rows
        within = global_rows % shard_rows
        is_cache = within < slot_count
        lengths_here = jnp.sum(
            jnp.where(owner_shard[:, None] == shard_ids[None, :], shard_lengths[None, :], 0), axis=1
        )
        token_number = owner_shard * token_count + (within - slot_count)
        allowed = jnp.where(
            is_cache[None, :],
            (within < lengths_here)[None, :],
            token_number[None, :] <= mine[:, None],
        )
        allowed = allowed[:, None, None, :]
        key_head_rows = key_block.reshape(-1, kv_heads, HEAD_SIZE)
        value_head_rows = value_block.reshape(-1, kv_heads, HEAD_SIZE)
        scores = (
            jnp.einsum("rhgd,khd->rhgk", grouped, key_head_rows, preferred_element_type=jnp.float32)
            * score_scale
        )
        new_high = jnp.maximum(highest, jnp.max(jnp.where(allowed, scores, -1e30), axis=-1))
        weights = jnp.where(allowed, jnp.exp(scores - new_high[..., None]), 0.0)
        fade = jnp.exp(highest - new_high)
        denominator = denominator * fade + jnp.sum(weights, axis=-1)
        product = jnp.einsum(
            "rhgk,khd->rhgd",
            weights.astype(jnp.bfloat16),
            value_head_rows,
            preferred_element_type=jnp.float32,
        )
        accum = accum * fade[..., None] + product
        return (new_high, denominator, accum)

    initial = (
        jnp.full((token_count, kv_heads, groups), -1e30, jnp.float32),
        jnp.zeros((token_count, kv_heads, groups), jnp.float32),
        jnp.zeros((token_count, kv_heads, groups, HEAD_SIZE), jnp.float32),
    )
    block_rows = shard_rows * 8

    def fold_pieces(state, pieces, start):
        key_piece, value_piece = pieces
        row_count = key_piece.shape[0]
        if row_count > block_rows and row_count % block_rows == 0:
            count = row_count // block_rows
            key_split = key_piece.reshape(count, block_rows, key_piece.shape[1])
            value_split = value_piece.reshape(count, block_rows, value_piece.shape[1])

            def inner(carry, items):
                key_one, value_one, number = items
                return (absorb(carry, key_one, value_one, start + number * block_rows), None)

            numbers = jnp.arange(count, dtype=jnp.int32)
            state, unused = lax.scan(inner, state, (key_split, value_split, numbers))
            return state
        return absorb(state, key_piece, value_piece, start)

    state = fold_pieces(
        initial,
        (
            lax.all_gather(key_here, "ctx", axis=0, tiled=True),
            lax.all_gather(value_here, "ctx", axis=0, tiled=True),
        ),
        jnp.int32(0),
    )
    highest, denominator, accum = state
    attended = accum / denominator[..., None]
    return attended.reshape(token_count, query_heads * HEAD_SIZE).astype(jnp.bfloat16)


MESH = pl.DeviceIdType.MESH


def turn_kernel(
    ctx_size, tp_size,
    owner_ref, lengths_ref, cosine_ref, sine_ref,
    hidden_ref, q_ref, down_ref, up_ref, keys_ref, values_ref, turn_keys_ref, turn_values_ref,
    out_ref,
    down_mine, down_pair, down_merged, down_cand,
    up_mine, up_pair, up_merged, up_cand,
    hid, base, cached_k, cached_v, fresh_k, fresh_v,
    partial, partials, low_mine, low_all, attended,
    pair_send, pair_recv, up_pair_send, up_pair_recv,
    column_send, column_recv, rows_send, rows_recv, part_send, part_recv,
    late_send, late_recv, local_sem,
):
    me = lax.axis_index("ctx")
    core = lax.axis_index("tp")
    column = lax.rem(me, 2)
    row = me // 2
    rows = ctx_size // 2
    slot = column * rows + row
    partner = me + 1 - 2 * column
    tokens = hidden_ref.shape[0]
    half = hidden_ref.shape[1] // tp_size
    chunk = half // ctx_size
    width = q_ref.shape[1] // ctx_size
    slots = keys_ref.shape[0]
    rank = down_ref.shape[0]

    barrier = pltpu.get_barrier_semaphore()
    for far in range(1, ctx_size * tp_size):
        other = lax.rem(me + far // tp_size, ctx_size)
        other_core = lax.rem(core + far % tp_size, tp_size)
        pl.semaphore_signal(
            barrier, inc=1, device_id={"ctx": other, "tp": other_core}, device_id_type=MESH
        )

    def slot_of(index):
        return lax.rem(index, 2) * rows + index // 2

    def features(number):
        return pl.ds(pl.multiple_of(core * half + number * chunk, chunk), chunk)

    def columns(number):
        return pl.ds(pl.multiple_of(number * width, width), width)

    def kv_columns(index):
        return pl.ds(pl.multiple_of(lax.rem(index, 2) * HEAD_SIZE, HEAD_SIZE), HEAD_SIZE)

    def block(index, size):
        return pl.ds(pl.multiple_of(index * size, size), size)

    local = []
    for far in range(rows):
        at = lax.rem(row + 1 + far, rows)
        local.append((down_ref.at[:, features(column * rows + at)], down_mine.at[at]))
        local.append((up_ref.at[:, columns(column * rows + at)], up_mine.at[at]))
    local.append((hidden_ref.at[:, features(slot)], hid.at[block(me, tokens)]))
    local.append((q_ref.at[:, columns(slot)], base.at[block(me, tokens)]))
    local.append((keys_ref.at[:, kv_columns(me)], cached_k.at[block(me, slots)]))
    local.append((values_ref.at[:, kv_columns(me)], cached_v.at[block(me, slots)]))
    local.append((turn_keys_ref.at[:, kv_columns(me)], fresh_k.at[block(me, tokens)]))
    local.append((turn_values_ref.at[:, kv_columns(me)], fresh_v.at[block(me, tokens)]))
    local = [
        pltpu.make_async_copy(source, target, local_sem.at[number])
        for number, (source, target) in enumerate(local)
    ]
    for copy in local:
        copy.start()

    pl.semaphore_wait(barrier, ctx_size * tp_size - 1)

    def remote(source, target, send, recv, index, to_core=None):
        return pltpu.make_async_remote_copy(
            src_ref=source, dst_ref=target, send_sem=send, recv_sem=recv,
            device_id={"ctx": index, "tp": core if to_core is None else to_core},
            device_id_type=MESH,
        )

    pair, up_copies = [], []
    for far in range(rows):
        at = lax.rem(row + 1 + far, rows)
        pair.append(remote(
            down_ref.at[:, features((1 - column) * rows + at)], down_pair.at[at],
            pair_send.at[far], pair_recv.at[far], partner,
        ))
        up_copies.append(remote(
            up_ref.at[:, columns((1 - column) * rows + at)], up_pair.at[at],
            up_pair_send.at[far], up_pair_recv.at[far], partner,
        ))
    for copy in pair:
        copy.start()

    moved = []
    for far in range(1, ctx_size):
        to = lax.rem(me + far, ctx_size)
        moved.append([
            remote(source, target, rows_send.at[kind, far], rows_recv.at[kind, far], to)
            for kind, (source, target) in enumerate([
                (hidden_ref.at[:, features(slot_of(to))], hid.at[block(me, tokens)]),
                (q_ref.at[:, columns(slot_of(to))], base.at[block(me, tokens)]),
                (keys_ref.at[:, kv_columns(to)], cached_k.at[block(me, slots)]),
                (values_ref.at[:, kv_columns(to)], cached_v.at[block(me, slots)]),
                (turn_keys_ref.at[:, kv_columns(to)], fresh_k.at[block(me, tokens)]),
                (turn_values_ref.at[:, kv_columns(to)], fresh_v.at[block(me, tokens)]),
            ])
        ])
    for copies in moved:
        copies[0].start()
    for copy in up_copies:
        copy.start()
    for kind in range(1, 6):
        for copies in moved:
            copies[kind].start()

    for copy in local:
        copy.wait()

    owner = owner_ref[0]
    owner_row = owner // 2
    is_mine = owner == me

    def merge(copies, mine, other, merged, cand, kind):
        sent = []
        for far in range(rows):
            at = lax.rem(row + 1 + far, rows)
            copies[far].wait_recv()
            chosen = lax.select_n(is_mine, other[at], mine[at])
            if far == rows - 1:
                cand[row] = chosen
            else:
                merged[at] = chosen
                copy = remote(
                    merged.at[at], cand.at[row],
                    column_send.at[kind, far], column_recv.at[kind, far], at * 2 + column,
                )
                copy.start()
                sent.append(copy)
        return sent

    down_sent = merge(pair, down_mine, down_pair, down_merged, down_cand, 0)
    up_sent = merge(up_copies, up_mine, up_pair, up_merged, up_cand, 1)
    for copies in moved:
        copies[0].wait_recv()
    for copy in down_sent:
        copy.wait_recv()

    product = lax.dot_general(
        hid[...], down_cand[owner_row], (((1,), (1,)), ((), ())),
        preferred_element_type=jnp.float32,
    )
    partial[...] = jnp.concatenate([product, jnp.zeros_like(product)], axis=1)
    summed = []
    mine_at = me * tp_size + core
    for far in range(1, ctx_size * tp_size):
        to = lax.rem(me + far // tp_size, ctx_size)
        copy = remote(
            partial.at[block(to, tokens)], partials.at[mine_at],
            part_send.at[far], part_recv.at[far], to,
            lax.rem(core + far % tp_size, tp_size),
        )
        copy.start()
        summed.append(copy)
    partials[mine_at] = partial[block(me, tokens)]
    for copy in summed:
        copy.wait_recv()
    total = partials[0]
    for number in range(1, ctx_size * tp_size):
        total = total + partials[number]
    lowrank = total.astype(jnp.bfloat16)
    low_mine[...] = lowrank
    low_all[block(me, tokens)] = lowrank
    low_sent = []
    for far in range(1, ctx_size):
        copy = remote(
            low_mine, low_all.at[block(me, tokens)],
            late_send.at[0, far], late_recv.at[0, far], lax.rem(me + far, ctx_size),
        )
        copy.start()
        low_sent.append(copy)

    for kind in range(1, 6):
        for copies in moved:
            copies[kind].wait_recv()
    for copy in up_sent:
        copy.wait_recv()
    cosine = cosine_ref[...]
    sine = sine_ref[...]

    def rotate(values):
        return values * cosine + pltpu.roll(values, HEAD_SIZE // 2, 1) * sine

    new_keys = rotate(fresh_k[...].astype(jnp.float32)).astype(jnp.bfloat16)
    new_values = fresh_v[...]
    old_keys = cached_k[...]
    old_values = cached_v[...]
    turn = tokens * ctx_size
    cache = slots * ctx_size
    place = lax.broadcasted_iota(jnp.int32, (turn, cache), 1)
    used = place < lengths_ref[0]
    for shard in range(1, ctx_size):
        begin = shard * slots
        used = used | ((place >= begin) & (place < begin + lengths_ref[shard]))
    token = lax.broadcasted_iota(jnp.int32, (turn, turn), 0)
    seen = lax.broadcasted_iota(jnp.int32, (turn, turn), 1) <= token
    scale = 1.0 / math.sqrt(HEAD_SIZE)

    for copy in low_sent:
        copy.wait_recv()
    delta = jnp.dot(
        low_all[:, :rank], up_cand[owner_row], preferred_element_type=jnp.float32
    )
    contract = (((1,), (1,)), ((), ()))
    for head in range(width // HEAD_SIZE):
        lanes = slice(head * HEAD_SIZE, (head + 1) * HEAD_SIZE)
        query = rotate(
            base[:, lanes].astype(jnp.float32) + 0.5 * delta[:, lanes]
        ).astype(jnp.bfloat16)
        old = lax.dot_general(query, old_keys, contract, preferred_element_type=jnp.float32)
        new = lax.dot_general(query, new_keys, contract, preferred_element_type=jnp.float32)
        old = jnp.where(used, old * scale, -1e30)
        new = jnp.where(seen, new * scale, -1e30)
        top = jnp.maximum(
            jnp.max(old, axis=1, keepdims=True), jnp.max(new, axis=1, keepdims=True)
        )
        old = jnp.where(used, jnp.exp(old - top), 0.0)
        new = jnp.where(seen, jnp.exp(new - top), 0.0)
        denominator = jnp.sum(old, axis=1, keepdims=True) + jnp.sum(new, axis=1, keepdims=True)
        gathered = jnp.dot(
            old.astype(jnp.bfloat16), old_values, preferred_element_type=jnp.float32
        ) + jnp.dot(new.astype(jnp.bfloat16), new_values, preferred_element_type=jnp.float32)
        attended[:, lanes] = (gathered / denominator).astype(jnp.bfloat16)

    sent = []
    for far in range(1, ctx_size):
        to = lax.rem(me + far, ctx_size)
        copy = remote(
            attended.at[block(to, tokens)], out_ref.at[:, columns(slot)],
            late_send.at[1, far], late_recv.at[1, far], to,
        )
        copy.start()
        sent.append(copy)
    out_ref[:, columns(slot)] = attended[block(me, tokens)]
    for copy in sent:
        copy.wait_recv()
    for copies in [pair, up_copies, down_sent, up_sent, summed, low_sent, sent] + moved:
        for copy in copies:
            copy.wait_send()


def turn_call(ctx_size, tp_size, *operands):
    (
        hidden, q_base, adapter_down, adapter_up, adapter_owner, turn_start, shard_lengths,
        stored_keys, stored_values, unrotated_turn_keys, incoming_values,
    ) = operands
    tokens, features = hidden.shape
    rank = adapter_down.shape[2]
    slots = stored_keys.shape[0]
    rows = ctx_size // 2
    chunk = features // tp_size // ctx_size
    width = q_base.shape[1] // ctx_size
    turn = tokens * ctx_size
    devices = ctx_size * tp_size
    half_dim = HEAD_SIZE // 2
    inverse = jnp.exp(
        jnp.arange(half_dim, dtype=jnp.float32) * (-2.0 * math.log(500000.0) / HEAD_SIZE)
    )
    positions = turn_start[0] + jnp.arange(turn, dtype=jnp.int32)
    angles = positions.astype(jnp.float32)[:, None] * inverse[None, :]
    cosine, sine = jnp.cos(angles), jnp.sin(angles)
    cosine = jnp.concatenate([cosine, cosine], axis=1)
    sine = jnp.concatenate([-sine, sine], axis=1)
    bf16, f32 = jnp.bfloat16, jnp.float32
    vmem, smem = pl.BlockSpec(memory_space=pltpu.VMEM), pl.BlockSpec(memory_space=pltpu.SMEM)
    anywhere = pl.BlockSpec(memory_space=pl.ANY)
    dma = pltpu.SemaphoreType.DMA
    return pl.pallas_call(
        functools.partial(turn_kernel, ctx_size, tp_size),
        out_shape=jax.ShapeDtypeStruct(q_base.shape, bf16),
        in_specs=[smem, smem, vmem, vmem] + [anywhere] * 8,
        out_specs=vmem,
        scratch_shapes=[pltpu.VMEM((rows, rank, chunk), bf16)] * 4
        + [pltpu.VMEM((rows, rank, width), bf16)] * 4
        + [
            pltpu.VMEM((turn, chunk), bf16),
            pltpu.VMEM((turn, width), bf16),
            pltpu.VMEM((slots * ctx_size, HEAD_SIZE), bf16),
            pltpu.VMEM((slots * ctx_size, HEAD_SIZE), bf16),
            pltpu.VMEM((turn, HEAD_SIZE), bf16),
            pltpu.VMEM((turn, HEAD_SIZE), bf16),
            pltpu.VMEM((turn, 2 * rank), f32),
            pltpu.VMEM((devices, tokens, 2 * rank), f32),
            pltpu.VMEM((tokens, 2 * rank), bf16),
            pltpu.VMEM((turn, 2 * rank), bf16),
            pltpu.VMEM((turn, width), bf16),
            dma((rows,)), dma((rows,)), dma((rows,)), dma((rows,)),
            dma((2, rows)), dma((2, rows)),
            dma((6, ctx_size)), dma((6, ctx_size)),
            dma((devices,)), dma((devices,)),
            dma((2, ctx_size)), dma((2, ctx_size)),
            dma((2 * rows + 6,)),
        ],
        compiler_params=pltpu.CompilerParams(
            collective_id=0, has_side_effects=True, vmem_limit_bytes=40 * 1024 * 1024
        ),
    )(
        adapter_owner, shard_lengths, cosine, sine,
        hidden, q_base, adapter_down[0].T, adapter_up[0],
        stored_keys, stored_values, unrotated_turn_keys, incoming_values,
    )


def program(mesh):
    ctx_size, tp_size = mesh.shape["ctx"], mesh.shape["tp"]

    def run(*operands):
        hidden, q_base, down, keys = operands[0], operands[1], operands[2], operands[7]
        fits = (
            ctx_size % 2 == 0
            and 4 <= ctx_size <= 16
            and keys.shape[1] == 2 * HEAD_SIZE
            and q_base.shape[1] % (ctx_size * HEAD_SIZE) == 0
            and hidden.shape[1] % (tp_size * ctx_size * 128) == 0
            and hidden.shape[0] % 16 == 0
            and keys.shape[0] % 16 == 0
            and 2 * down.shape[2] == 128
        )
        if fits:
            return turn_call(ctx_size, tp_size, *operands)
        return shards(*operands)

    return run


def solution(mesh):
    return jax.shard_map(
        program(mesh),
        mesh=mesh,
        in_specs=(
            P(("group", "ctx"), None),
            P(("group", "ctx"), "tp"),
            P(("group", "ctx"), None, None),
            P(("group", "ctx"), None, "tp"),
            P("group"),
            P("group"),
            P("group"),
            P(("group", "ctx"), "tp"),
            P(("group", "ctx"), "tp"),
            P(("group", "ctx"), "tp"),
            P(("group", "ctx"), "tp"),
        ),
        out_specs=P(("group", "ctx"), "tp"),
        check_vma=False,
    )
```

```python
import functools
import math

import jax
import jax.numpy as jnp
from jax import lax
from jax.experimental import pallas as pl
from jax.experimental.pallas import tpu as pltpu
from jax.sharding import PartitionSpec as P

HEAD_SIZE = 128


def spread(shard, axis, root):
    mine = lax.axis_index(axis) == root
    return lax.psum(jnp.where(mine, shard, jnp.zeros_like(shard)), axis)


def apply_rotary(values, token_positions, heads):
    half_dim = HEAD_SIZE // 2
    inverse = jnp.exp(
        jnp.arange(half_dim, dtype=jnp.float32) * (-2.0 * math.log(500000.0) / HEAD_SIZE)
    )
    angles = token_positions.astype(jnp.float32)[:, None] * inverse[None, :]
    cosine = jnp.cos(angles)[:, None, :]
    sine = jnp.sin(angles)[:, None, :]
    shaped = values.reshape(values.shape[0], heads, HEAD_SIZE)
    first = shaped[..., :half_dim]
    second = shaped[..., half_dim:]
    turned = jnp.concatenate(
        [first * cosine - second * sine, second * cosine + first * sine], axis=-1
    )
    return turned.reshape(values.shape[0], heads * HEAD_SIZE)


def shards(
    hidden,
    q_base,
    adapter_down,
    adapter_up,
    adapter_owner,
    turn_start,
    shard_lengths,
    stored_keys,
    stored_values,
    unrotated_turn_keys,
    incoming_values,
):
    holder = adapter_owner[0]
    slot_down = adapter_down[0]
    slot_up = adapter_up[0]
    got_down, got_up = (spread(slot_down, "ctx", holder), spread(slot_up, "ctx", holder))
    lowrank = jnp.dot(hidden, got_down, preferred_element_type=jnp.float32).astype(jnp.bfloat16)
    adapter_delta = jnp.dot(lowrank, got_up, preferred_element_type=jnp.float32)
    token_count = q_base.shape[0]
    slot_count = stored_keys.shape[0]
    shard_rows = token_count + slot_count
    ctx_size = lax.axis_size("ctx")
    myself = lax.axis_index("ctx")
    query_heads = q_base.shape[1] // HEAD_SIZE
    kv_heads = unrotated_turn_keys.shape[1] // HEAD_SIZE
    groups = query_heads // kv_heads
    local_tokens = jnp.arange(token_count, dtype=jnp.int32)
    token_positions = turn_start[0] + myself * token_count + local_tokens
    query_rows = apply_rotary(
        q_base.astype(jnp.float32) + 0.5 * adapter_delta, token_positions, query_heads
    ).astype(jnp.bfloat16)
    rotated_turn_keys = apply_rotary(
        unrotated_turn_keys.astype(jnp.float32), token_positions, kv_heads
    ).astype(jnp.bfloat16)
    grouped = query_rows.reshape(token_count, kv_heads, groups, HEAD_SIZE)
    key_here = jnp.concatenate([stored_keys, rotated_turn_keys], axis=0)
    value_here = jnp.concatenate([stored_values, incoming_values], axis=0)
    mine = myself * token_count + local_tokens
    score_scale = 1.0 / math.sqrt(HEAD_SIZE)
    shard_ids = jnp.arange(ctx_size, dtype=jnp.int32)

    def absorb(state, key_block, value_block, start):
        highest, denominator, accum = state
        row_count = key_block.shape[0]
        global_rows = start + jnp.arange(row_count, dtype=jnp.int32)
        owner_shard = global_rows // shard_rows
        within = global_rows % shard_rows
        is_cache = within < slot_count
        lengths_here = jnp.sum(
            jnp.where(owner_shard[:, None] == shard_ids[None, :], shard_lengths[None, :], 0), axis=1
        )
        token_number = owner_shard * token_count + (within - slot_count)
        allowed = jnp.where(
            is_cache[None, :],
            (within < lengths_here)[None, :],
            token_number[None, :] <= mine[:, None],
        )
        allowed = allowed[:, None, None, :]
        key_head_rows = key_block.reshape(-1, kv_heads, HEAD_SIZE)
        value_head_rows = value_block.reshape(-1, kv_heads, HEAD_SIZE)
        scores = (
            jnp.einsum("rhgd,khd->rhgk", grouped, key_head_rows, preferred_element_type=jnp.float32)
            * score_scale
        )
        new_high = jnp.maximum(highest, jnp.max(jnp.where(allowed, scores, -1e30), axis=-1))
        weights = jnp.where(allowed, jnp.exp(scores - new_high[..., None]), 0.0)
        fade = jnp.exp(highest - new_high)
        denominator = denominator * fade + jnp.sum(weights, axis=-1)
        product = jnp.einsum(
            "rhgk,khd->rhgd",
            weights.astype(jnp.bfloat16),
            value_head_rows,
            preferred_element_type=jnp.float32,
        )
        accum = accum * fade[..., None] + product
        return (new_high, denominator, accum)

    initial = (
        jnp.full((token_count, kv_heads, groups), -1e30, jnp.float32),
        jnp.zeros((token_count, kv_heads, groups), jnp.float32),
        jnp.zeros((token_count, kv_heads, groups, HEAD_SIZE), jnp.float32),
    )
    block_rows = shard_rows * 8

    def fold_pieces(state, pieces, start):
        key_piece, value_piece = pieces
        row_count = key_piece.shape[0]
        if row_count > block_rows and row_count % block_rows == 0:
            count = row_count // block_rows
            key_split = key_piece.reshape(count, block_rows, key_piece.shape[1])
            value_split = value_piece.reshape(count, block_rows, value_piece.shape[1])

            def inner(carry, items):
                key_one, value_one, number = items
                return (absorb(carry, key_one, value_one, start + number * block_rows), None)

            numbers = jnp.arange(count, dtype=jnp.int32)
            state, unused = lax.scan(inner, state, (key_split, value_split, numbers))
            return state
        return absorb(state, key_piece, value_piece, start)

    state = fold_pieces(
        initial,
        (
            lax.all_gather(key_here, "ctx", axis=0, tiled=True),
            lax.all_gather(value_here, "ctx", axis=0, tiled=True),
        ),
        jnp.int32(0),
    )
    highest, denominator, accum = state
    attended = accum / denominator[..., None]
    return attended.reshape(token_count, query_heads * HEAD_SIZE).astype(jnp.bfloat16)


MESH = pl.DeviceIdType.MESH


def turn_kernel(
    ctx_size, tp_size,
    owner_ref, lengths_ref, cosine_ref, sine_ref,
    hidden_ref, q_ref, down_ref, up_ref, keys_ref, values_ref, turn_keys_ref, turn_values_ref,
    out_ref,
    down_mine, down_pair, down_merged, down_cand,
    up_mine, up_pair, up_merged, up_cand,
    hid, base, cached_k, cached_v, fresh_k, fresh_v,
    partial, partials, low_mine, low_all, attended,
    pair_send, pair_recv, up_pair_send, up_pair_recv,
    column_send, column_recv, rows_send, rows_recv, part_send, part_recv,
    late_send, late_recv, local_sem,
):
    me = lax.axis_index("ctx")
    core = lax.axis_index("tp")
    column = lax.rem(me, 2)
    row = me // 2
    rows = ctx_size // 2
    slot = column * rows + row
    partner = me + 1 - 2 * column
    tokens = hidden_ref.shape[0]
    half = hidden_ref.shape[1] // tp_size
    chunk = half // ctx_size
    width = q_ref.shape[1] // ctx_size
    slots = keys_ref.shape[0]
    rank = down_ref.shape[0]

    barrier = pltpu.get_barrier_semaphore()
    for far in range(1, ctx_size * tp_size):
        other = lax.rem(me + far // tp_size, ctx_size)
        other_core = lax.rem(core + far % tp_size, tp_size)
        pl.semaphore_signal(
            barrier, inc=1, device_id={"ctx": other, "tp": other_core}, device_id_type=MESH
        )

    def slot_of(index):
        return lax.rem(index, 2) * rows + index // 2

    def features(number):
        return pl.ds(pl.multiple_of(core * half + number * chunk, chunk), chunk)

    def columns(number):
        return pl.ds(pl.multiple_of(number * width, width), width)

    def kv_columns(index):
        return pl.ds(pl.multiple_of(lax.rem(index, 2) * HEAD_SIZE, HEAD_SIZE), HEAD_SIZE)

    def block(index, size):
        return pl.ds(pl.multiple_of(index * size, size), size)

    local = []
    for far in range(rows):
        at = lax.rem(row + 1 + far, rows)
        local.append((down_ref.at[:, features(column * rows + at)], down_mine.at[at]))
        local.append((up_ref.at[:, columns(column * rows + at)], up_mine.at[at]))
    local.append((hidden_ref.at[:, features(slot)], hid.at[block(me, tokens)]))
    local.append((q_ref.at[:, columns(slot)], base.at[block(me, tokens)]))
    local.append((keys_ref.at[:, kv_columns(me)], cached_k.at[block(me, slots)]))
    local.append((values_ref.at[:, kv_columns(me)], cached_v.at[block(me, slots)]))
    local.append((turn_keys_ref.at[:, kv_columns(me)], fresh_k.at[block(me, tokens)]))
    local.append((turn_values_ref.at[:, kv_columns(me)], fresh_v.at[block(me, tokens)]))
    local = [
        pltpu.make_async_copy(source, target, local_sem.at[number])
        for number, (source, target) in enumerate(local)
    ]
    for copy in local:
        copy.start()

    pl.semaphore_wait(barrier, ctx_size * tp_size - 1)

    def remote(source, target, send, recv, index, to_core=None):
        return pltpu.make_async_remote_copy(
            src_ref=source, dst_ref=target, send_sem=send, recv_sem=recv,
            device_id={"ctx": index, "tp": core if to_core is None else to_core},
            device_id_type=MESH,
        )

    pair, up_copies = [], []
    for far in range(rows):
        at = lax.rem(row + 1 + far, rows)
        pair.append(remote(
            down_ref.at[:, features((1 - column) * rows + at)], down_pair.at[at],
            pair_send.at[far], pair_recv.at[far], partner,
        ))
        up_copies.append(remote(
            up_ref.at[:, columns((1 - column) * rows + at)], up_pair.at[at],
            up_pair_send.at[far], up_pair_recv.at[far], partner,
        ))
    for copy in pair:
        copy.start()

    moved = []
    for far in range(1, ctx_size):
        to = lax.rem(me + far, ctx_size)
        moved.append([
            remote(source, target, rows_send.at[kind, far], rows_recv.at[kind, far], to)
            for kind, (source, target) in enumerate([
                (hidden_ref.at[:, features(slot_of(to))], hid.at[block(me, tokens)]),
                (q_ref.at[:, columns(slot_of(to))], base.at[block(me, tokens)]),
                (keys_ref.at[:, kv_columns(to)], cached_k.at[block(me, slots)]),
                (values_ref.at[:, kv_columns(to)], cached_v.at[block(me, slots)]),
                (turn_keys_ref.at[:, kv_columns(to)], fresh_k.at[block(me, tokens)]),
                (turn_values_ref.at[:, kv_columns(to)], fresh_v.at[block(me, tokens)]),
            ])
        ])
    for copies in moved:
        copies[0].start()
    for copy in local:
        copy.wait()

    owner = owner_ref[0]
    owner_row = owner // 2
    is_mine = owner == me

    def merge(copies, mine, other, merged, cand, kind):
        sent = []
        for far in range(rows):
            at = lax.rem(row + 1 + far, rows)
            copies[far].wait_recv()
            chosen = lax.select_n(is_mine, other[at], mine[at])
            if far == rows - 1:
                cand[row] = chosen
            else:
                merged[at] = chosen
                copy = remote(
                    merged.at[at], cand.at[row],
                    column_send.at[kind, far], column_recv.at[kind, far], at * 2 + column,
                )
                copy.start()
                sent.append(copy)
        return sent

    down_sent = merge(pair, down_mine, down_pair, down_merged, down_cand, 0)
    for copy in up_copies:
        copy.start()
    for kind in range(1, 6):
        for copies in moved:
            copies[kind].start()
    for copies in moved:
        copies[0].wait_recv()
    for copy in down_sent:
        copy.wait_recv()

    product = lax.dot_general(
        hid[...], down_cand[owner_row], (((1,), (1,)), ((), ())),
        preferred_element_type=jnp.float32,
    )
    partial[...] = jnp.concatenate([product, jnp.zeros_like(product)], axis=1)
    summed = []
    mine_at = me * tp_size + core
    for far in range(1, ctx_size * tp_size):
        to = lax.rem(me + far // tp_size, ctx_size)
        copy = remote(
            partial.at[block(to, tokens)], partials.at[mine_at],
            part_send.at[far], part_recv.at[far], to,
            lax.rem(core + far % tp_size, tp_size),
        )
        copy.start()
        summed.append(copy)
    partials[mine_at] = partial[block(me, tokens)]
    up_sent = merge(up_copies, up_mine, up_pair, up_merged, up_cand, 1)
    for copy in summed:
        copy.wait_recv()
    total = partials[0]
    for number in range(1, ctx_size * tp_size):
        total = total + partials[number]
    lowrank = total.astype(jnp.bfloat16)
    low_mine[...] = lowrank
    low_all[block(me, tokens)] = lowrank
    low_sent = []
    for far in range(1, ctx_size):
        copy = remote(
            low_mine, low_all.at[block(me, tokens)],
            late_send.at[0, far], late_recv.at[0, far], lax.rem(me + far, ctx_size),
        )
        copy.start()
        low_sent.append(copy)

    for kind in range(1, 6):
        for copies in moved:
            copies[kind].wait_recv()
    for copy in up_sent:
        copy.wait_recv()
    cosine = cosine_ref[...]
    sine = sine_ref[...]

    def rotate(values):
        return values * cosine + pltpu.roll(values, HEAD_SIZE // 2, 1) * sine

    new_keys = rotate(fresh_k[...].astype(jnp.float32)).astype(jnp.bfloat16)
    new_values = fresh_v[...]
    old_keys = cached_k[...]
    old_values = cached_v[...]
    turn = tokens * ctx_size
    cache = slots * ctx_size
    place = lax.broadcasted_iota(jnp.int32, (turn, cache), 1)
    used = place < lengths_ref[0]
    for shard in range(1, ctx_size):
        begin = shard * slots
        used = used | ((place >= begin) & (place < begin + lengths_ref[shard]))
    token = lax.broadcasted_iota(jnp.int32, (turn, turn), 0)
    seen = lax.broadcasted_iota(jnp.int32, (turn, turn), 1) <= token
    scale = 1.0 / math.sqrt(HEAD_SIZE)

    for copy in low_sent:
        copy.wait_recv()
    delta = jnp.dot(
        low_all[:, :rank], up_cand[owner_row], preferred_element_type=jnp.float32
    )
    contract = (((1,), (1,)), ((), ()))
    for head in range(width // HEAD_SIZE):
        lanes = slice(head * HEAD_SIZE, (head + 1) * HEAD_SIZE)
        query = rotate(
            base[:, lanes].astype(jnp.float32) + 0.5 * delta[:, lanes]
        ).astype(jnp.bfloat16)
        old = lax.dot_general(query, old_keys, contract, preferred_element_type=jnp.float32)
        new = lax.dot_general(query, new_keys, contract, preferred_element_type=jnp.float32)
        old = jnp.where(used, old * scale, -1e30)
        new = jnp.where(seen, new * scale, -1e30)
        top = jnp.maximum(
            jnp.max(old, axis=1, keepdims=True), jnp.max(new, axis=1, keepdims=True)
        )
        old = jnp.where(used, jnp.exp(old - top), 0.0)
        new = jnp.where(seen, jnp.exp(new - top), 0.0)
        denominator = jnp.sum(old, axis=1, keepdims=True) + jnp.sum(new, axis=1, keepdims=True)
        gathered = jnp.dot(
            old.astype(jnp.bfloat16), old_values, preferred_element_type=jnp.float32
        ) + jnp.dot(new.astype(jnp.bfloat16), new_values, preferred_element_type=jnp.float32)
        attended[:, lanes] = (gathered / denominator).astype(jnp.bfloat16)

    sent = []
    for far in range(1, ctx_size):
        to = lax.rem(me + far, ctx_size)
        copy = remote(
            attended.at[block(to, tokens)], out_ref.at[:, columns(slot)],
            late_send.at[1, far], late_recv.at[1, far], to,
        )
        copy.start()
        sent.append(copy)
    out_ref[:, columns(slot)] = attended[block(me, tokens)]
    for copy in sent:
        copy.wait_recv()
    for copies in [pair, up_copies, down_sent, up_sent, summed, low_sent, sent] + moved:
        for copy in copies:
            copy.wait_send()


def turn_call(ctx_size, tp_size, *operands):
    (
        hidden, q_base, adapter_down, adapter_up, adapter_owner, turn_start, shard_lengths,
        stored_keys, stored_values, unrotated_turn_keys, incoming_values,
    ) = operands
    tokens, features = hidden.shape
    rank = adapter_down.shape[2]
    slots = stored_keys.shape[0]
    rows = ctx_size // 2
    chunk = features // tp_size // ctx_size
    width = q_base.shape[1] // ctx_size
    turn = tokens * ctx_size
    devices = ctx_size * tp_size
    half_dim = HEAD_SIZE // 2
    inverse = jnp.exp(
        jnp.arange(half_dim, dtype=jnp.float32) * (-2.0 * math.log(500000.0) / HEAD_SIZE)
    )
    positions = turn_start[0] + jnp.arange(turn, dtype=jnp.int32)
    angles = positions.astype(jnp.float32)[:, None] * inverse[None, :]
    cosine, sine = jnp.cos(angles), jnp.sin(angles)
    cosine = jnp.concatenate([cosine, cosine], axis=1)
    sine = jnp.concatenate([-sine, sine], axis=1)
    bf16, f32 = jnp.bfloat16, jnp.float32
    vmem, smem = pl.BlockSpec(memory_space=pltpu.VMEM), pl.BlockSpec(memory_space=pltpu.SMEM)
    anywhere = pl.BlockSpec(memory_space=pltpu.HBM)
    dma = pltpu.SemaphoreType.DMA
    return pl.pallas_call(
        functools.partial(turn_kernel, ctx_size, tp_size),
        out_shape=jax.ShapeDtypeStruct(q_base.shape, bf16),
        in_specs=[smem, smem, vmem, vmem] + [anywhere] * 8,
        out_specs=vmem,
        scratch_shapes=[pltpu.VMEM((rows, rank, chunk), bf16)] * 4
        + [pltpu.VMEM((rows, rank, width), bf16)] * 4
        + [
            pltpu.VMEM((turn, chunk), bf16),
            pltpu.VMEM((turn, width), bf16),
            pltpu.VMEM((slots * ctx_size, HEAD_SIZE), bf16),
            pltpu.VMEM((slots * ctx_size, HEAD_SIZE), bf16),
            pltpu.VMEM((turn, HEAD_SIZE), bf16),
            pltpu.VMEM((turn, HEAD_SIZE), bf16),
            pltpu.VMEM((turn, 2 * rank), f32),
            pltpu.VMEM((devices, tokens, 2 * rank), f32),
            pltpu.VMEM((tokens, 2 * rank), bf16),
            pltpu.VMEM((turn, 2 * rank), bf16),
            pltpu.VMEM((turn, width), bf16),
            dma((rows,)), dma((rows,)), dma((rows,)), dma((rows,)),
            dma((2, rows)), dma((2, rows)),
            dma((6, ctx_size)), dma((6, ctx_size)),
            dma((devices,)), dma((devices,)),
            dma((2, ctx_size)), dma((2, ctx_size)),
            dma((2 * rows + 6,)),
        ],
        compiler_params=pltpu.CompilerParams(
            collective_id=0, has_side_effects=True, vmem_limit_bytes=40 * 1024 * 1024
        ),
    )(
        adapter_owner, shard_lengths, cosine, sine,
        hidden, q_base, adapter_down[0].T, adapter_up[0],
        stored_keys, stored_values, unrotated_turn_keys, incoming_values,
    )


def program(mesh):
    ctx_size, tp_size = mesh.shape["ctx"], mesh.shape["tp"]

    def run(*operands):
        hidden, q_base, down, keys = operands[0], operands[1], operands[2], operands[7]
        fits = (
            ctx_size % 2 == 0
            and 4 <= ctx_size <= 16
            and keys.shape[1] == 2 * HEAD_SIZE
            and q_base.shape[1] % (ctx_size * HEAD_SIZE) == 0
            and hidden.shape[1] % (tp_size * ctx_size * 128) == 0
            and hidden.shape[0] % 16 == 0
            and keys.shape[0] % 16 == 0
            and 2 * down.shape[2] == 128
        )
        if fits:
            return turn_call(ctx_size, tp_size, *operands)
        return shards(*operands)

    return run


def solution(mesh):
    return jax.shard_map(
        program(mesh),
        mesh=mesh,
        in_specs=(
            P(("group", "ctx"), None),
            P(("group", "ctx"), "tp"),
            P(("group", "ctx"), None, None),
            P(("group", "ctx"), None, "tp"),
            P("group"),
            P("group"),
            P("group"),
            P(("group", "ctx"), "tp"),
            P(("group", "ctx"), "tp"),
            P(("group", "ctx"), "tp"),
            P(("group", "ctx"), "tp"),
        ),
        out_specs=P(("group", "ctx"), "tp"),
        check_vma=False,
    )
```

```python
import functools
import math

import jax
import jax.numpy as jnp
from jax import lax
from jax.experimental import pallas as pl
from jax.experimental.pallas import tpu as pltpu
from jax.sharding import PartitionSpec as P

HEAD_SIZE = 128


def spread(shard, axis, root):
    mine = lax.axis_index(axis) == root
    return lax.psum(jnp.where(mine, shard, jnp.zeros_like(shard)), axis)


def apply_rotary(values, token_positions, heads):
    half_dim = HEAD_SIZE // 2
    inverse = jnp.exp(
        jnp.arange(half_dim, dtype=jnp.float32) * (-2.0 * math.log(500000.0) / HEAD_SIZE)
    )
    angles = token_positions.astype(jnp.float32)[:, None] * inverse[None, :]
    cosine = jnp.cos(angles)[:, None, :]
    sine = jnp.sin(angles)[:, None, :]
    shaped = values.reshape(values.shape[0], heads, HEAD_SIZE)
    first = shaped[..., :half_dim]
    second = shaped[..., half_dim:]
    turned = jnp.concatenate(
        [first * cosine - second * sine, second * cosine + first * sine], axis=-1
    )
    return turned.reshape(values.shape[0], heads * HEAD_SIZE)


def shards(
    hidden,
    q_base,
    adapter_down,
    adapter_up,
    adapter_owner,
    turn_start,
    shard_lengths,
    stored_keys,
    stored_values,
    unrotated_turn_keys,
    incoming_values,
):
    holder = adapter_owner[0]
    slot_down = adapter_down[0]
    slot_up = adapter_up[0]
    got_down, got_up = (spread(slot_down, "ctx", holder), spread(slot_up, "ctx", holder))
    lowrank = jnp.dot(hidden, got_down, preferred_element_type=jnp.float32).astype(jnp.bfloat16)
    adapter_delta = jnp.dot(lowrank, got_up, preferred_element_type=jnp.float32)
    token_count = q_base.shape[0]
    slot_count = stored_keys.shape[0]
    shard_rows = token_count + slot_count
    ctx_size = lax.axis_size("ctx")
    myself = lax.axis_index("ctx")
    query_heads = q_base.shape[1] // HEAD_SIZE
    kv_heads = unrotated_turn_keys.shape[1] // HEAD_SIZE
    groups = query_heads // kv_heads
    local_tokens = jnp.arange(token_count, dtype=jnp.int32)
    token_positions = turn_start[0] + myself * token_count + local_tokens
    query_rows = apply_rotary(
        q_base.astype(jnp.float32) + 0.5 * adapter_delta, token_positions, query_heads
    ).astype(jnp.bfloat16)
    rotated_turn_keys = apply_rotary(
        unrotated_turn_keys.astype(jnp.float32), token_positions, kv_heads
    ).astype(jnp.bfloat16)
    grouped = query_rows.reshape(token_count, kv_heads, groups, HEAD_SIZE)
    key_here = jnp.concatenate([stored_keys, rotated_turn_keys], axis=0)
    value_here = jnp.concatenate([stored_values, incoming_values], axis=0)
    mine = myself * token_count + local_tokens
    score_scale = 1.0 / math.sqrt(HEAD_SIZE)
    shard_ids = jnp.arange(ctx_size, dtype=jnp.int32)

    def absorb(state, key_block, value_block, start):
        highest, denominator, accum = state
        row_count = key_block.shape[0]
        global_rows = start + jnp.arange(row_count, dtype=jnp.int32)
        owner_shard = global_rows // shard_rows
        within = global_rows % shard_rows
        is_cache = within < slot_count
        lengths_here = jnp.sum(
            jnp.where(owner_shard[:, None] == shard_ids[None, :], shard_lengths[None, :], 0), axis=1
        )
        token_number = owner_shard * token_count + (within - slot_count)
        allowed = jnp.where(
            is_cache[None, :],
            (within < lengths_here)[None, :],
            token_number[None, :] <= mine[:, None],
        )
        allowed = allowed[:, None, None, :]
        key_head_rows = key_block.reshape(-1, kv_heads, HEAD_SIZE)
        value_head_rows = value_block.reshape(-1, kv_heads, HEAD_SIZE)
        scores = (
            jnp.einsum("rhgd,khd->rhgk", grouped, key_head_rows, preferred_element_type=jnp.float32)
            * score_scale
        )
        new_high = jnp.maximum(highest, jnp.max(jnp.where(allowed, scores, -1e30), axis=-1))
        weights = jnp.where(allowed, jnp.exp(scores - new_high[..., None]), 0.0)
        fade = jnp.exp(highest - new_high)
        denominator = denominator * fade + jnp.sum(weights, axis=-1)
        product = jnp.einsum(
            "rhgk,khd->rhgd",
            weights.astype(jnp.bfloat16),
            value_head_rows,
            preferred_element_type=jnp.float32,
        )
        accum = accum * fade[..., None] + product
        return (new_high, denominator, accum)

    initial = (
        jnp.full((token_count, kv_heads, groups), -1e30, jnp.float32),
        jnp.zeros((token_count, kv_heads, groups), jnp.float32),
        jnp.zeros((token_count, kv_heads, groups, HEAD_SIZE), jnp.float32),
    )
    block_rows = shard_rows * 8

    def fold_pieces(state, pieces, start):
        key_piece, value_piece = pieces
        row_count = key_piece.shape[0]
        if row_count > block_rows and row_count % block_rows == 0:
            count = row_count // block_rows
            key_split = key_piece.reshape(count, block_rows, key_piece.shape[1])
            value_split = value_piece.reshape(count, block_rows, value_piece.shape[1])

            def inner(carry, items):
                key_one, value_one, number = items
                return (absorb(carry, key_one, value_one, start + number * block_rows), None)

            numbers = jnp.arange(count, dtype=jnp.int32)
            state, unused = lax.scan(inner, state, (key_split, value_split, numbers))
            return state
        return absorb(state, key_piece, value_piece, start)

    state = fold_pieces(
        initial,
        (
            lax.all_gather(key_here, "ctx", axis=0, tiled=True),
            lax.all_gather(value_here, "ctx", axis=0, tiled=True),
        ),
        jnp.int32(0),
    )
    highest, denominator, accum = state
    attended = accum / denominator[..., None]
    return attended.reshape(token_count, query_heads * HEAD_SIZE).astype(jnp.bfloat16)


MESH = pl.DeviceIdType.MESH


def turn_kernel(
    ctx_size, tp_size,
    owner_ref, lengths_ref, cosine_ref, sine_ref,
    hidden_ref, q_ref, down_ref, up_ref, keys_ref, values_ref, turn_keys_ref, turn_values_ref,
    out_ref,
    down_mine, down_pair, down_merged, down_cand,
    up_mine, up_pair, up_merged, up_cand,
    hid, base, cached_k, cached_v, fresh_k, fresh_v,
    partial, partials, low_mine, low_all, attended,
    pair_send, pair_recv, up_pair_send, up_pair_recv,
    column_send, column_recv, rows_send, rows_recv, part_send, part_recv,
    late_send, late_recv, local_sem,
):
    me = lax.axis_index("ctx")
    core = lax.axis_index("tp")
    column = lax.rem(me, 2)
    row = me // 2
    rows = ctx_size // 2
    slot = column * rows + row
    partner = me + 1 - 2 * column
    tokens = hidden_ref.shape[0]
    half = hidden_ref.shape[1] // tp_size
    chunk = half // ctx_size
    width = q_ref.shape[1] // ctx_size
    slots = keys_ref.shape[0]
    rank = down_ref.shape[0]

    barrier = pltpu.get_barrier_semaphore()
    for far in range(1, ctx_size * tp_size):
        other = lax.rem(me + far // tp_size, ctx_size)
        other_core = lax.rem(core + far % tp_size, tp_size)
        pl.semaphore_signal(
            barrier, inc=1, device_id={"ctx": other, "tp": other_core}, device_id_type=MESH
        )

    def slot_of(index):
        return lax.rem(index, 2) * rows + index // 2

    def features(number):
        return pl.ds(pl.multiple_of(core * half + number * chunk, chunk), chunk)

    def columns(number):
        return pl.ds(pl.multiple_of(number * width, width), width)

    def kv_columns(index):
        return pl.ds(pl.multiple_of(lax.rem(index, 2) * HEAD_SIZE, HEAD_SIZE), HEAD_SIZE)

    def block(index, size):
        return pl.ds(pl.multiple_of(index * size, size), size)

    local = []
    for far in range(rows):
        at = lax.rem(row + 1 + far, rows)
        local.append((down_ref.at[:, features(column * rows + at)], down_mine.at[at]))
        local.append((up_ref.at[:, columns(column * rows + at)], up_mine.at[at]))
    local.append((hidden_ref.at[:, features(slot)], hid.at[block(me, tokens)]))
    local.append((q_ref.at[:, columns(slot)], base.at[block(me, tokens)]))
    local.append((keys_ref.at[:, kv_columns(me)], cached_k.at[block(me, slots)]))
    local.append((values_ref.at[:, kv_columns(me)], cached_v.at[block(me, slots)]))
    local.append((turn_keys_ref.at[:, kv_columns(me)], fresh_k.at[block(me, tokens)]))
    local.append((turn_values_ref.at[:, kv_columns(me)], fresh_v.at[block(me, tokens)]))
    local = [
        pltpu.make_async_copy(source, target, local_sem.at[number])
        for number, (source, target) in enumerate(local)
    ]
    for copy in local:
        copy.start()

    pl.semaphore_wait(barrier, ctx_size * tp_size - 1)

    def remote(source, target, send, recv, index, to_core=None):
        return pltpu.make_async_remote_copy(
            src_ref=source, dst_ref=target, send_sem=send, recv_sem=recv,
            device_id={"ctx": index, "tp": core if to_core is None else to_core},
            device_id_type=MESH,
        )

    pair, up_copies = [], []
    for far in range(rows):
        at = lax.rem(row + 1 + far, rows)
        pair.append(remote(
            down_ref.at[:, features((1 - column) * rows + at)], down_pair.at[at],
            pair_send.at[far], pair_recv.at[far], partner,
        ))
        up_copies.append(remote(
            up_ref.at[:, columns((1 - column) * rows + at)], up_pair.at[at],
            up_pair_send.at[far], up_pair_recv.at[far], partner,
        ))
    for copy in pair:
        copy.start()

    moved = []
    for far in range(1, ctx_size):
        to = lax.rem(me + far, ctx_size)
        moved.append([
            remote(source, target, rows_send.at[kind, far], rows_recv.at[kind, far], to)
            for kind, (source, target) in enumerate([
                (hidden_ref.at[:, features(slot_of(to))], hid.at[block(me, tokens)]),
                (q_ref.at[:, columns(slot_of(to))], base.at[block(me, tokens)]),
                (keys_ref.at[:, kv_columns(to)], cached_k.at[block(me, slots)]),
                (values_ref.at[:, kv_columns(to)], cached_v.at[block(me, slots)]),
                (turn_keys_ref.at[:, kv_columns(to)], fresh_k.at[block(me, tokens)]),
                (turn_values_ref.at[:, kv_columns(to)], fresh_v.at[block(me, tokens)]),
            ])
        ])
    for copies in moved:
        copies[0].start()
    for copy in local:
        copy.wait()

    owner = owner_ref[0]
    owner_row = owner // 2
    is_mine = owner == me

    def merge(copies, mine, other, merged, cand, kind):
        sent = []
        for far in range(rows):
            at = lax.rem(row + 1 + far, rows)
            copies[far].wait_recv()
            chosen = lax.select_n(is_mine, other[at], mine[at])
            if far == rows - 1:
                cand[row] = chosen
            else:
                merged[at] = chosen
                copy = remote(
                    merged.at[at], cand.at[row],
                    column_send.at[kind, far], column_recv.at[kind, far], at * 2 + column,
                )
                copy.start()
                sent.append(copy)
        return sent

    down_sent = merge(pair, down_mine, down_pair, down_merged, down_cand, 0)
    for copy in up_copies:
        copy.start()
    for kind in range(1, 6):
        for copies in moved:
            copies[kind].start()
    for copies in moved:
        copies[0].wait_recv()
    for copy in down_sent:
        copy.wait_recv()

    product = lax.dot_general(
        hid[...], down_cand[owner_row], (((1,), (1,)), ((), ())),
        preferred_element_type=jnp.float32,
    )
    partial[...] = jnp.concatenate([product, jnp.zeros_like(product)], axis=1)
    summed = []
    mine_at = me * tp_size + core
    for far in range(1, ctx_size * tp_size):
        to = lax.rem(me + far // tp_size, ctx_size)
        copy = remote(
            partial.at[block(to, tokens)], partials.at[mine_at],
            part_send.at[far], part_recv.at[far], to,
            lax.rem(core + far % tp_size, tp_size),
        )
        copy.start()
        summed.append(copy)
    partials[mine_at] = partial[block(me, tokens)]
    up_sent = merge(up_copies, up_mine, up_pair, up_merged, up_cand, 1)
    for copy in summed:
        copy.wait_recv()
    total = partials[0]
    for number in range(1, ctx_size * tp_size):
        total = total + partials[number]
    lowrank = total.astype(jnp.bfloat16)
    low_mine[...] = lowrank
    low_all[block(me, tokens)] = lowrank
    low_sent = []
    for far in range(1, ctx_size):
        copy = remote(
            low_mine, low_all.at[block(me, tokens)],
            late_send.at[0, far], late_recv.at[0, far], lax.rem(me + far, ctx_size),
        )
        copy.start()
        low_sent.append(copy)

    for kind in range(1, 6):
        for copies in moved:
            copies[kind].wait_recv()
    for copy in up_sent:
        copy.wait_recv()
    cosine = cosine_ref[...]
    sine = sine_ref[...]

    def rotate(values):
        return values * cosine + pltpu.roll(values, HEAD_SIZE // 2, 1) * sine

    new_keys = rotate(fresh_k[...].astype(jnp.float32)).astype(jnp.bfloat16)
    new_values = fresh_v[...]
    old_keys = cached_k[...]
    old_values = cached_v[...]
    turn = tokens * ctx_size
    cache = slots * ctx_size
    place = lax.broadcasted_iota(jnp.int32, (turn, cache), 1)
    used = place < lengths_ref[0]
    for shard in range(1, ctx_size):
        begin = shard * slots
        used = used | ((place >= begin) & (place < begin + lengths_ref[shard]))
    token = lax.broadcasted_iota(jnp.int32, (turn, turn), 0)
    seen = lax.broadcasted_iota(jnp.int32, (turn, turn), 1) <= token
    scale = 1.0 / math.sqrt(HEAD_SIZE)

    for copy in low_sent:
        copy.wait_recv()
    delta = jnp.dot(
        low_all[:, :rank], up_cand[owner_row], preferred_element_type=jnp.float32
    )
    contract = (((1,), (1,)), ((), ()))
    sent = []
    for head in range(width // HEAD_SIZE):
        lanes = slice(head * HEAD_SIZE, (head + 1) * HEAD_SIZE)
        query = rotate(
            base[:, lanes].astype(jnp.float32) + 0.5 * delta[:, lanes]
        ).astype(jnp.bfloat16)
        old = lax.dot_general(query, old_keys, contract, preferred_element_type=jnp.float32)
        new = lax.dot_general(query, new_keys, contract, preferred_element_type=jnp.float32)
        old = jnp.where(used, old * scale, -1e30)
        new = jnp.where(seen, new * scale, -1e30)
        top = jnp.maximum(
            jnp.max(old, axis=1, keepdims=True), jnp.max(new, axis=1, keepdims=True)
        )
        old = jnp.where(used, jnp.exp(old - top), 0.0)
        new = jnp.where(seen, jnp.exp(new - top), 0.0)
        denominator = jnp.sum(old, axis=1, keepdims=True) + jnp.sum(new, axis=1, keepdims=True)
        gathered = jnp.dot(
            old.astype(jnp.bfloat16), old_values, preferred_element_type=jnp.float32
        ) + jnp.dot(new.astype(jnp.bfloat16), new_values, preferred_element_type=jnp.float32)
        attended[:, lanes] = (gathered / denominator).astype(jnp.bfloat16)
        out_lanes = pl.ds(
            pl.multiple_of(slot * width + head * HEAD_SIZE, HEAD_SIZE), HEAD_SIZE
        )
        for far in range(1, ctx_size):
            to = lax.rem(me + far, ctx_size)
            copy = remote(
                attended.at[block(to, tokens), lanes], out_ref.at[:, out_lanes],
                late_send.at[1 + head, far], late_recv.at[1 + head, far], to,
            )
            copy.start()
            sent.append(copy)
    out_ref[:, columns(slot)] = attended[block(me, tokens)]
    for copy in sent:
        copy.wait_recv()
    for copies in [pair, up_copies, down_sent, up_sent, summed, low_sent, sent] + moved:
        for copy in copies:
            copy.wait_send()


def turn_call(ctx_size, tp_size, *operands):
    (
        hidden, q_base, adapter_down, adapter_up, adapter_owner, turn_start, shard_lengths,
        stored_keys, stored_values, unrotated_turn_keys, incoming_values,
    ) = operands
    tokens, features = hidden.shape
    rank = adapter_down.shape[2]
    slots = stored_keys.shape[0]
    rows = ctx_size // 2
    chunk = features // tp_size // ctx_size
    width = q_base.shape[1] // ctx_size
    turn = tokens * ctx_size
    devices = ctx_size * tp_size
    half_dim = HEAD_SIZE // 2
    inverse = jnp.exp(
        jnp.arange(half_dim, dtype=jnp.float32) * (-2.0 * math.log(500000.0) / HEAD_SIZE)
    )
    positions = turn_start[0] + jnp.arange(turn, dtype=jnp.int32)
    angles = positions.astype(jnp.float32)[:, None] * inverse[None, :]
    cosine, sine = jnp.cos(angles), jnp.sin(angles)
    cosine = jnp.concatenate([cosine, cosine], axis=1)
    sine = jnp.concatenate([-sine, sine], axis=1)
    bf16, f32 = jnp.bfloat16, jnp.float32
    vmem, smem = pl.BlockSpec(memory_space=pltpu.VMEM), pl.BlockSpec(memory_space=pltpu.SMEM)
    anywhere = pl.BlockSpec(memory_space=pltpu.HBM)
    dma = pltpu.SemaphoreType.DMA
    return pl.pallas_call(
        functools.partial(turn_kernel, ctx_size, tp_size),
        out_shape=jax.ShapeDtypeStruct(q_base.shape, bf16),
        in_specs=[smem, smem, vmem, vmem] + [anywhere] * 8,
        out_specs=vmem,
        scratch_shapes=[pltpu.VMEM((rows, rank, chunk), bf16)] * 4
        + [pltpu.VMEM((rows, rank, width), bf16)] * 4
        + [
            pltpu.VMEM((turn, chunk), bf16),
            pltpu.VMEM((turn, width), bf16),
            pltpu.VMEM((slots * ctx_size, HEAD_SIZE), bf16),
            pltpu.VMEM((slots * ctx_size, HEAD_SIZE), bf16),
            pltpu.VMEM((turn, HEAD_SIZE), bf16),
            pltpu.VMEM((turn, HEAD_SIZE), bf16),
            pltpu.VMEM((turn, 2 * rank), f32),
            pltpu.VMEM((devices, tokens, 2 * rank), f32),
            pltpu.VMEM((tokens, 2 * rank), bf16),
            pltpu.VMEM((turn, 2 * rank), bf16),
            pltpu.VMEM((turn, width), bf16),
            dma((rows,)), dma((rows,)), dma((rows,)), dma((rows,)),
            dma((2, rows)), dma((2, rows)),
            dma((6, ctx_size)), dma((6, ctx_size)),
            dma((devices,)), dma((devices,)),
            dma((1 + width // HEAD_SIZE, ctx_size)), dma((1 + width // HEAD_SIZE, ctx_size)),
            dma((2 * rows + 6,)),
        ],
        compiler_params=pltpu.CompilerParams(
            collective_id=0, has_side_effects=True, vmem_limit_bytes=62 * 1024 * 1024
        ),
    )(
        adapter_owner, shard_lengths, cosine, sine,
        hidden, q_base, adapter_down[0].T, adapter_up[0],
        stored_keys, stored_values, unrotated_turn_keys, incoming_values,
    )


def program(mesh):
    ctx_size, tp_size = mesh.shape["ctx"], mesh.shape["tp"]

    def run(*operands):
        hidden, q_base, down, keys = operands[0], operands[1], operands[2], operands[7]
        fits = (
            ctx_size % 2 == 0
            and 4 <= ctx_size <= 16
            and keys.shape[1] == 2 * HEAD_SIZE
            and q_base.shape[1] % (ctx_size * HEAD_SIZE) == 0
            and hidden.shape[1] % (tp_size * ctx_size * 128) == 0
            and hidden.shape[0] % 16 == 0
            and keys.shape[0] % 16 == 0
            and 2 * down.shape[2] == 128
        )
        if fits:
            return turn_call(ctx_size, tp_size, *operands)
        return shards(*operands)

    return run


def solution(mesh):
    return jax.shard_map(
        program(mesh),
        mesh=mesh,
        in_specs=(
            P(("group", "ctx"), None),
            P(("group", "ctx"), "tp"),
            P(("group", "ctx"), None, None),
            P(("group", "ctx"), None, "tp"),
            P("group"),
            P("group"),
            P("group"),
            P(("group", "ctx"), "tp"),
            P(("group", "ctx"), "tp"),
            P(("group", "ctx"), "tp"),
            P(("group", "ctx"), "tp"),
        ),
        out_specs=P(("group", "ctx"), "tp"),
        check_vma=False,
    )
```

```python
import functools
import math

import jax
import jax.numpy as jnp
from jax import lax
from jax.experimental import pallas as pl
from jax.experimental.pallas import tpu as pltpu
from jax.sharding import PartitionSpec as P

HEAD_SIZE = 128


def spread(shard, axis, root):
    mine = lax.axis_index(axis) == root
    return lax.psum(jnp.where(mine, shard, jnp.zeros_like(shard)), axis)


def apply_rotary(values, token_positions, heads):
    half_dim = HEAD_SIZE // 2
    inverse = jnp.exp(
        jnp.arange(half_dim, dtype=jnp.float32) * (-2.0 * math.log(500000.0) / HEAD_SIZE)
    )
    angles = token_positions.astype(jnp.float32)[:, None] * inverse[None, :]
    cosine = jnp.cos(angles)[:, None, :]
    sine = jnp.sin(angles)[:, None, :]
    shaped = values.reshape(values.shape[0], heads, HEAD_SIZE)
    first = shaped[..., :half_dim]
    second = shaped[..., half_dim:]
    turned = jnp.concatenate(
        [first * cosine - second * sine, second * cosine + first * sine], axis=-1
    )
    return turned.reshape(values.shape[0], heads * HEAD_SIZE)


def shards(
    hidden,
    q_base,
    adapter_down,
    adapter_up,
    adapter_owner,
    turn_start,
    shard_lengths,
    stored_keys,
    stored_values,
    unrotated_turn_keys,
    incoming_values,
):
    holder = adapter_owner[0]
    slot_down = adapter_down[0]
    slot_up = adapter_up[0]
    got_down, got_up = (spread(slot_down, "ctx", holder), spread(slot_up, "ctx", holder))
    lowrank = jnp.dot(hidden, got_down, preferred_element_type=jnp.float32).astype(jnp.bfloat16)
    adapter_delta = jnp.dot(lowrank, got_up, preferred_element_type=jnp.float32)
    token_count = q_base.shape[0]
    slot_count = stored_keys.shape[0]
    shard_rows = token_count + slot_count
    ctx_size = lax.axis_size("ctx")
    myself = lax.axis_index("ctx")
    query_heads = q_base.shape[1] // HEAD_SIZE
    kv_heads = unrotated_turn_keys.shape[1] // HEAD_SIZE
    groups = query_heads // kv_heads
    local_tokens = jnp.arange(token_count, dtype=jnp.int32)
    token_positions = turn_start[0] + myself * token_count + local_tokens
    query_rows = apply_rotary(
        q_base.astype(jnp.float32) + 0.5 * adapter_delta, token_positions, query_heads
    ).astype(jnp.bfloat16)
    rotated_turn_keys = apply_rotary(
        unrotated_turn_keys.astype(jnp.float32), token_positions, kv_heads
    ).astype(jnp.bfloat16)
    grouped = query_rows.reshape(token_count, kv_heads, groups, HEAD_SIZE)
    key_here = jnp.concatenate([stored_keys, rotated_turn_keys], axis=0)
    value_here = jnp.concatenate([stored_values, incoming_values], axis=0)
    mine = myself * token_count + local_tokens
    score_scale = 1.0 / math.sqrt(HEAD_SIZE)
    shard_ids = jnp.arange(ctx_size, dtype=jnp.int32)

    def absorb(state, key_block, value_block, start):
        highest, denominator, accum = state
        row_count = key_block.shape[0]
        global_rows = start + jnp.arange(row_count, dtype=jnp.int32)
        owner_shard = global_rows // shard_rows
        within = global_rows % shard_rows
        is_cache = within < slot_count
        lengths_here = jnp.sum(
            jnp.where(owner_shard[:, None] == shard_ids[None, :], shard_lengths[None, :], 0), axis=1
        )
        token_number = owner_shard * token_count + (within - slot_count)
        allowed = jnp.where(
            is_cache[None, :],
            (within < lengths_here)[None, :],
            token_number[None, :] <= mine[:, None],
        )
        allowed = allowed[:, None, None, :]
        key_head_rows = key_block.reshape(-1, kv_heads, HEAD_SIZE)
        value_head_rows = value_block.reshape(-1, kv_heads, HEAD_SIZE)
        scores = (
            jnp.einsum("rhgd,khd->rhgk", grouped, key_head_rows, preferred_element_type=jnp.float32)
            * score_scale
        )
        new_high = jnp.maximum(highest, jnp.max(jnp.where(allowed, scores, -1e30), axis=-1))
        weights = jnp.where(allowed, jnp.exp(scores - new_high[..., None]), 0.0)
        fade = jnp.exp(highest - new_high)
        denominator = denominator * fade + jnp.sum(weights, axis=-1)
        product = jnp.einsum(
            "rhgk,khd->rhgd",
            weights.astype(jnp.bfloat16),
            value_head_rows,
            preferred_element_type=jnp.float32,
        )
        accum = accum * fade[..., None] + product
        return (new_high, denominator, accum)

    initial = (
        jnp.full((token_count, kv_heads, groups), -1e30, jnp.float32),
        jnp.zeros((token_count, kv_heads, groups), jnp.float32),
        jnp.zeros((token_count, kv_heads, groups, HEAD_SIZE), jnp.float32),
    )
    block_rows = shard_rows * 8

    def fold_pieces(state, pieces, start):
        key_piece, value_piece = pieces
        row_count = key_piece.shape[0]
        if row_count > block_rows and row_count % block_rows == 0:
            count = row_count // block_rows
            key_split = key_piece.reshape(count, block_rows, key_piece.shape[1])
            value_split = value_piece.reshape(count, block_rows, value_piece.shape[1])

            def inner(carry, items):
                key_one, value_one, number = items
                return (absorb(carry, key_one, value_one, start + number * block_rows), None)

            numbers = jnp.arange(count, dtype=jnp.int32)
            state, unused = lax.scan(inner, state, (key_split, value_split, numbers))
            return state
        return absorb(state, key_piece, value_piece, start)

    state = fold_pieces(
        initial,
        (
            lax.all_gather(key_here, "ctx", axis=0, tiled=True),
            lax.all_gather(value_here, "ctx", axis=0, tiled=True),
        ),
        jnp.int32(0),
    )
    highest, denominator, accum = state
    attended = accum / denominator[..., None]
    return attended.reshape(token_count, query_heads * HEAD_SIZE).astype(jnp.bfloat16)


MESH = pl.DeviceIdType.MESH


def turn_kernel(
    ctx_size, tp_size,
    owner_ref, lengths_ref, cosine_ref, sine_ref,
    hidden_ref, q_ref, down_ref, up_ref, keys_ref, values_ref, turn_keys_ref, turn_values_ref,
    out_ref,
    down_mine, down_pair, down_merged, down_cand,
    up_mine, up_pair, up_merged, up_cand,
    hid, base, cached_k, cached_v, fresh_k, fresh_v,
    partial, partials, low_mine, low_all, attended,
    pair_send, pair_recv, up_pair_send, up_pair_recv,
    column_send, column_recv, rows_send, rows_recv, part_send, part_recv,
    late_send, late_recv, local_sem,
):
    me = lax.axis_index("ctx")
    core = lax.axis_index("tp")
    column = lax.rem(me, 2)
    row = me // 2
    rows = ctx_size // 2
    slot = column * rows + row
    partner = me + 1 - 2 * column
    tokens = hidden_ref.shape[0]
    half = hidden_ref.shape[1] // tp_size
    chunk = half // ctx_size
    width = q_ref.shape[1] // ctx_size
    slots = keys_ref.shape[0]
    rank = down_ref.shape[0]

    barrier = pltpu.get_barrier_semaphore()
    for far in range(1, ctx_size * tp_size):
        other = lax.rem(me + far // tp_size, ctx_size)
        other_core = lax.rem(core + far % tp_size, tp_size)
        pl.semaphore_signal(
            barrier, inc=1, device_id={"ctx": other, "tp": other_core}, device_id_type=MESH
        )

    def slot_of(index):
        return lax.rem(index, 2) * rows + index // 2

    def features(number):
        return pl.ds(pl.multiple_of(core * half + number * chunk, chunk), chunk)

    def columns(number):
        return pl.ds(pl.multiple_of(number * width, width), width)

    def kv_columns(index):
        return pl.ds(pl.multiple_of(lax.rem(index, 2) * HEAD_SIZE, HEAD_SIZE), HEAD_SIZE)

    def block(index, size):
        return pl.ds(pl.multiple_of(index * size, size), size)

    local = []
    for far in range(rows):
        at = lax.rem(row + 1 + far, rows)
        local.append((down_ref.at[:, features(column * rows + at)], down_mine.at[at]))
        local.append((up_ref.at[:, columns(column * rows + at)], up_mine.at[at]))
    local.append((hidden_ref.at[:, features(slot)], hid.at[block(me, tokens)]))
    local.append((q_ref.at[:, columns(slot)], base.at[block(me, tokens)]))
    local.append((keys_ref.at[:, kv_columns(me)], cached_k.at[block(me, slots)]))
    local.append((values_ref.at[:, kv_columns(me)], cached_v.at[block(me, slots)]))
    local.append((turn_keys_ref.at[:, kv_columns(me)], fresh_k.at[block(me, tokens)]))
    local.append((turn_values_ref.at[:, kv_columns(me)], fresh_v.at[block(me, tokens)]))
    local = [
        pltpu.make_async_copy(source, target, local_sem.at[number])
        for number, (source, target) in enumerate(local)
    ]
    for copy in local:
        copy.start()

    pl.semaphore_wait(barrier, ctx_size * tp_size - 1)

    def remote(source, target, send, recv, index, to_core=None):
        return pltpu.make_async_remote_copy(
            src_ref=source, dst_ref=target, send_sem=send, recv_sem=recv,
            device_id={"ctx": index, "tp": core if to_core is None else to_core},
            device_id_type=MESH,
        )

    pair, up_copies = [], []
    for far in range(rows):
        at = lax.rem(row + 1 + far, rows)
        pair.append(remote(
            down_ref.at[:, features((1 - column) * rows + at)], down_pair.at[at],
            pair_send.at[far], pair_recv.at[far], partner,
        ))
        up_copies.append(remote(
            up_ref.at[:, columns((1 - column) * rows + at)], up_pair.at[at],
            up_pair_send.at[far], up_pair_recv.at[far], partner,
        ))
    for far in (0, 2, 1, 3):
        pair[far].start()

    moved = []
    for far in range(1, ctx_size):
        to = lax.rem(me + far, ctx_size)
        moved.append([
            remote(source, target, rows_send.at[kind, far], rows_recv.at[kind, far], to)
            for kind, (source, target) in enumerate([
                (hidden_ref.at[:, features(slot_of(to))], hid.at[block(me, tokens)]),
                (q_ref.at[:, columns(slot_of(to))], base.at[block(me, tokens)]),
                (keys_ref.at[:, kv_columns(to)], cached_k.at[block(me, slots)]),
                (values_ref.at[:, kv_columns(to)], cached_v.at[block(me, slots)]),
                (turn_keys_ref.at[:, kv_columns(to)], fresh_k.at[block(me, tokens)]),
                (turn_values_ref.at[:, kv_columns(to)], fresh_v.at[block(me, tokens)]),
            ])
        ])
    for copies in moved:
        copies[0].start()
    for copy in local:
        copy.wait()

    owner = owner_ref[0]
    owner_row = owner // 2
    is_mine = owner == me

    near = row + 1 - 2 * lax.rem(row, 2)
    far_row = lax.rem(row + 2, rows)
    in_row = owner_row == row
    in_half = owner_row // 2 == row // 2

    def merge_near(copies, mine, other, merged, cand, kind):
        sent = []
        for far in (0, 2, 1, 3):
            at = lax.rem(row + 1 + far, rows)
            copies[far].wait_recv()
            merged[at] = lax.select_n(is_mine, other[at], mine[at])
            if far % 2 == 0:
                copy = remote(
                    merged.at[at], cand.at[at // 2],
                    column_send.at[kind, at // 2], column_recv.at[kind, at // 2],
                    near * 2 + column,
                )
                copy.start()
                sent.append(copy)
        return sent

    def merge_far(sent, merged, cand, kind):
        for copy in sent:
            copy.wait_recv()
        merged[far_row] = lax.select_n(in_row, cand[far_row // 2], merged[far_row])
        copy = remote(
            merged.at[far_row], cand.at[2],
            column_send.at[kind, 2], column_recv.at[kind, 2], far_row * 2 + column,
        )
        copy.start()
        cand[3] = lax.select_n(in_row, cand[row // 2], merged[row])
        return copy

    down_sent = merge_near(pair, down_mine, down_pair, down_merged, down_cand, 0)
    for far in (0, 2, 1, 3):
        up_copies[far].start()
    for kind in range(1, 6):
        for copies in moved:
            copies[kind].start()
    down_last = merge_far(down_sent, down_merged, down_cand, 0)
    for copies in moved:
        copies[0].wait_recv()
    down_last.wait_recv()

    product = lax.dot_general(
        hid[...], lax.select_n(in_half, down_cand[2], down_cand[3]), (((1,), (1,)), ((), ())),
        preferred_element_type=jnp.float32,
    )
    split = tokens // 2
    for index in range(ctx_size):
        first = index * tokens
        partial[index * split : (index + 1) * split] = jnp.concatenate(
            [product[first : first + split], product[first + split : first + tokens]], axis=1
        )
    summed = []
    mine_at = me * tp_size + core
    for far in range(1, ctx_size * tp_size):
        to = lax.rem(me + far // tp_size, ctx_size)
        copy = remote(
            partial.at[block(to, split)], partials.at[mine_at],
            part_send.at[far], part_recv.at[far], to,
            lax.rem(core + far % tp_size, tp_size),
        )
        copy.start()
        summed.append(copy)
    partials[mine_at] = partial[block(me, split)]
    up_sent = merge_near(up_copies, up_mine, up_pair, up_merged, up_cand, 1)
    for copy in summed:
        copy.wait_recv()
    total = partials[0]
    for number in range(1, ctx_size * tp_size):
        total = total + partials[number]
    lowrank = jnp.concatenate([total[:, :rank], total[:, rank:]], axis=0)
    lowrank = jnp.concatenate([lowrank, lowrank], axis=1).astype(jnp.bfloat16)
    low_mine[...] = lowrank
    low_all[block(me, tokens)] = lowrank
    low_sent = []
    for far in range(1, ctx_size):
        copy = remote(
            low_mine, low_all.at[block(me, tokens)],
            late_send.at[0, far], late_recv.at[0, far], lax.rem(me + far, ctx_size),
        )
        copy.start()
        low_sent.append(copy)

    up_last = merge_far(up_sent, up_merged, up_cand, 1)
    for kind in range(1, 6):
        for copies in moved:
            copies[kind].wait_recv()
    cosine = cosine_ref[...]
    sine = sine_ref[...]

    def rotate(values):
        return values * cosine + pltpu.roll(values, HEAD_SIZE // 2, 1) * sine

    new_keys = rotate(fresh_k[...].astype(jnp.float32)).astype(jnp.bfloat16)
    new_values = fresh_v[...]
    old_keys = cached_k[...]
    old_values = cached_v[...]
    turn = tokens * ctx_size
    cache = slots * ctx_size
    place = lax.broadcasted_iota(jnp.int32, (turn, cache), 1)
    used = place < lengths_ref[0]
    for shard in range(1, ctx_size):
        begin = shard * slots
        used = used | ((place >= begin) & (place < begin + lengths_ref[shard]))
    token = lax.broadcasted_iota(jnp.int32, (turn, turn), 0)
    seen = lax.broadcasted_iota(jnp.int32, (turn, turn), 1) <= token
    scale = 1.0 / math.sqrt(HEAD_SIZE)

    for copy in low_sent:
        copy.wait_recv()
    up_last.wait_recv()
    delta = jnp.dot(
        low_all[:, :rank], lax.select_n(in_half, up_cand[2], up_cand[3]), preferred_element_type=jnp.float32
    )
    contract = (((1,), (1,)), ((), ()))
    sent = []
    for head in range(width // HEAD_SIZE):
        lanes = slice(head * HEAD_SIZE, (head + 1) * HEAD_SIZE)
        query = rotate(
            base[:, lanes].astype(jnp.float32) + 0.5 * delta[:, lanes]
        ).astype(jnp.bfloat16)
        old = lax.dot_general(query, old_keys, contract, preferred_element_type=jnp.float32)
        new = lax.dot_general(query, new_keys, contract, preferred_element_type=jnp.float32)
        old = jnp.where(used, old * scale, -1e30)
        new = jnp.where(seen, new * scale, -1e30)
        top = jnp.maximum(
            jnp.max(old, axis=1, keepdims=True), jnp.max(new, axis=1, keepdims=True)
        )
        old = jnp.where(used, jnp.exp(old - top), 0.0)
        new = jnp.where(seen, jnp.exp(new - top), 0.0)
        denominator = jnp.sum(old, axis=1, keepdims=True) + jnp.sum(new, axis=1, keepdims=True)
        gathered = jnp.dot(
            old.astype(jnp.bfloat16), old_values, preferred_element_type=jnp.float32
        ) + jnp.dot(new.astype(jnp.bfloat16), new_values, preferred_element_type=jnp.float32)
        attended[:, lanes] = (gathered / denominator).astype(jnp.bfloat16)
        out_lanes = pl.ds(
            pl.multiple_of(slot * width + head * HEAD_SIZE, HEAD_SIZE), HEAD_SIZE
        )
        for far in range(1, ctx_size):
            to = lax.rem(me + far, ctx_size)
            copy = remote(
                attended.at[block(to, tokens), lanes], out_ref.at[:, out_lanes],
                late_send.at[1 + head, far], late_recv.at[1 + head, far], to,
            )
            copy.start()
            sent.append(copy)
    out_ref[:, columns(slot)] = attended[block(me, tokens)]
    for copy in sent:
        copy.wait_recv()
    for copies in [pair, up_copies, down_sent, up_sent, [down_last, up_last], summed, low_sent, sent] + moved:
        for copy in copies:
            copy.wait_send()


def turn_call(ctx_size, tp_size, *operands):
    (
        hidden, q_base, adapter_down, adapter_up, adapter_owner, turn_start, shard_lengths,
        stored_keys, stored_values, unrotated_turn_keys, incoming_values,
    ) = operands
    tokens, features = hidden.shape
    rank = adapter_down.shape[2]
    slots = stored_keys.shape[0]
    rows = ctx_size // 2
    chunk = features // tp_size // ctx_size
    width = q_base.shape[1] // ctx_size
    turn = tokens * ctx_size
    devices = ctx_size * tp_size
    half_dim = HEAD_SIZE // 2
    inverse = jnp.exp(
        jnp.arange(half_dim, dtype=jnp.float32) * (-2.0 * math.log(500000.0) / HEAD_SIZE)
    )
    positions = turn_start[0] + jnp.arange(turn, dtype=jnp.int32)
    angles = positions.astype(jnp.float32)[:, None] * inverse[None, :]
    cosine, sine = jnp.cos(angles), jnp.sin(angles)
    cosine = jnp.concatenate([cosine, cosine], axis=1)
    sine = jnp.concatenate([-sine, sine], axis=1)
    bf16, f32 = jnp.bfloat16, jnp.float32
    vmem, smem = pl.BlockSpec(memory_space=pltpu.VMEM), pl.BlockSpec(memory_space=pltpu.SMEM)
    anywhere = pl.BlockSpec(memory_space=pltpu.HBM)
    dma = pltpu.SemaphoreType.DMA
    return pl.pallas_call(
        functools.partial(turn_kernel, ctx_size, tp_size),
        out_shape=jax.ShapeDtypeStruct(q_base.shape, bf16),
        in_specs=[smem, smem, vmem, vmem] + [anywhere] * 8,
        out_specs=vmem,
        scratch_shapes=[pltpu.VMEM((rows, rank, chunk), bf16)] * 4
        + [pltpu.VMEM((rows, rank, width), bf16)] * 4
        + [
            pltpu.VMEM((turn, chunk), bf16),
            pltpu.VMEM((turn, width), bf16),
            pltpu.VMEM((slots * ctx_size, HEAD_SIZE), bf16),
            pltpu.VMEM((slots * ctx_size, HEAD_SIZE), bf16),
            pltpu.VMEM((turn, HEAD_SIZE), bf16),
            pltpu.VMEM((turn, HEAD_SIZE), bf16),
            pltpu.VMEM((turn // 2, 2 * rank), f32),
            pltpu.VMEM((devices, tokens // 2, 2 * rank), f32),
            pltpu.VMEM((tokens, 2 * rank), bf16),
            pltpu.VMEM((turn, 2 * rank), bf16),
            pltpu.VMEM((turn, width), bf16),
            dma((rows,)), dma((rows,)), dma((rows,)), dma((rows,)),
            dma((2, rows)), dma((2, rows)),
            dma((6, ctx_size)), dma((6, ctx_size)),
            dma((devices,)), dma((devices,)),
            dma((1 + width // HEAD_SIZE, ctx_size)), dma((1 + width // HEAD_SIZE, ctx_size)),
            dma((2 * rows + 6,)),
        ],
        compiler_params=pltpu.CompilerParams(
            collective_id=0, has_side_effects=True, vmem_limit_bytes=62 * 1024 * 1024
        ),
    )(
        adapter_owner, shard_lengths, cosine, sine,
        hidden, q_base, adapter_down[0].T, adapter_up[0],
        stored_keys, stored_values, unrotated_turn_keys, incoming_values,
    )


def program(mesh):
    ctx_size, tp_size = mesh.shape["ctx"], mesh.shape["tp"]

    def run(*operands):
        hidden, q_base, down, keys = operands[0], operands[1], operands[2], operands[7]
        fits = (
            ctx_size % 2 == 0
            and ctx_size == 8
            and keys.shape[1] == 2 * HEAD_SIZE
            and q_base.shape[1] % (ctx_size * HEAD_SIZE) == 0
            and hidden.shape[1] % (tp_size * ctx_size * 128) == 0
            and hidden.shape[0] % 16 == 0
            and keys.shape[0] % 16 == 0
            and 2 * down.shape[2] == 128
        )
        if fits:
            return turn_call(ctx_size, tp_size, *operands)
        return shards(*operands)

    return run


def solution(mesh):
    return jax.shard_map(
        program(mesh),
        mesh=mesh,
        in_specs=(
            P(("group", "ctx"), None),
            P(("group", "ctx"), "tp"),
            P(("group", "ctx"), None, None),
            P(("group", "ctx"), None, "tp"),
            P("group"),
            P("group"),
            P("group"),
            P(("group", "ctx"), "tp"),
            P(("group", "ctx"), "tp"),
            P(("group", "ctx"), "tp"),
            P(("group", "ctx"), "tp"),
        ),
        out_specs=P(("group", "ctx"), "tp"),
        check_vma=False,
    )
```
